32 devices in a mesh: groups: 2 (over x), blk: 16 (over z, y, core).
Axes of the slice: x: 2, y: 2, z: 4, core: 2. Of those that a mesh axis runs over, the one named last changes fastest.
Arguments:
- query_grads: bfloat16 [3584, 65536], P(('groups', 'blk')), parts along dimension 0, may hold values from -6 to 6
- train_grads: bfloat16 [256, 65536], P(('groups', 'blk')), parts along dimension 0, may hold values from -6 to 6
- basis_out: bfloat16 [256, 256], replicated, may hold values from -0.375 to 0.375
- basis_in: bfloat16 [256, 256], replicated, may hold values from -0.375 to 0.375
- eigen_out: float32 [256], replicated, may hold values from 0.3 to 3
- eigen_in: float32 [256], replicated, may hold values from 0.3 to 3
Outputs:
- influence: float32 [3584, 128], P(('groups', 'blk')), parts along dimension 0
- train_totals: float32 [256], P(('groups', 'blk')), parts along dimension 0
The draws below stay inside these ranges and needn't reach their ends.
There are 2 independent parts, one for each index of `groups`. The reference program is written for one: setup_inputs(seed, part) draws one part's arguments, and reference() takes and returns one part's arrays. A program takes and returns all parts, laid end to end along the dimension named above; an argument that names none is the same for every part. Nothing has to cross between parts.
All inputs are finite; a program needn't handle non-finite values.
Results may differ from the reference program's by a relative error of at most 0.0041.
Values may be sent and summed in bfloat16 or wider, within the bound.
A program may use at most 192 MiB of HBM per device.

```python
import math
import jax
import jax.numpy as jnp
from jax import lax

R = 256
G = 65536
QDEV = 112
QUERIES = 1792
TRAIN = 128


def steps_of(stream_key, extent, cuts, smallest, high):
    def one(position, blocks):
        heights = jax.random.uniform(jax.random.fold_in(jax.random.fold_in(stream_key, 6), position), (blocks,), jnp.float32, smallest / len(cuts), high / len(cuts))
        return jnp.repeat(jnp.exp(heights), extent[position] // blocks).reshape((-1,) + (1,) * (len(extent) - position - 1))

    factor_of = one(*cuts[0])
    for cut in cuts[1:]:
        factor_of = factor_of * one(*cut)
    return factor_of


def normal_values(rng, extent, scale, bound, pieces=(), held_as=jnp.bfloat16):
    loudness = steps_of(rng, extent, pieces, -0.22, 0.18) if pieces else 1.0
    result = jax.random.normal(rng, extent, jnp.float32) * scale * loudness
    return jnp.minimum(jnp.maximum(result, -bound), bound).astype(held_as)


def setup_inputs(seed: int = 0, part: int = 0) -> dict:
    key_of = jax.random.split(jax.random.key(seed), 7)
    own_keys = jax.random.split(jax.random.fold_in(key_of[6], part), 7)
    return {
        "query_grads": normal_values(own_keys[0], (QUERIES, G), 1.0, 6.0, ((0, 16),)),
        "train_grads": normal_values(own_keys[1], (TRAIN, G), 1.0, 6.0, ((0, 16),)),
        "basis_out": normal_values(key_of[2], (R, R), R ** -0.5, 0.375),
        "basis_in": normal_values(key_of[3], (R, R), R ** -0.5, 0.375),
        "eigen_out": jnp.clip(jnp.exp(jax.random.uniform(key_of[4], (R,), jnp.float32, math.log(0.3), math.log(3.0))), 0.3, 3.0),
        "eigen_in": jnp.clip(jnp.exp(jax.random.uniform(key_of[5], (R,), jnp.float32, math.log(0.3), math.log(3.0))), 0.3, 3.0),
    }


damping = 0.1

def rotate(gradients, basis_out, basis_in, weights):
    count = gradients.shape[0]
    half = jnp.dot(gradients.reshape(count * R, R), basis_in, preferred_element_type=jnp.float32).astype(jnp.bfloat16)
    half = half.reshape(count, R, R).astype(jnp.float32)
    turned = jnp.einsum('ai,naj->nij', basis_out.astype(jnp.float32), half, precision=lax.Precision.HIGHEST)
    if weights is not None:
        turned = turned * weights
    return turned.astype(jnp.bfloat16).reshape(count, R * R)

def reference(query_grads, train_grads, basis_out, basis_in, eigen_out, eigen_in):
    weights = 1.0 / (eigen_out[:, None] * eigen_in[None, :] + damping)
    train_eigen = rotate(train_grads, basis_out, basis_in, None)
    shards = query_grads.reshape(QUERIES // QDEV, QDEV, R * R)

    def score_shard(shard):
        query_eigen = rotate(shard, basis_out, basis_in, weights)
        raw = lax.dot_general(query_eigen, train_eigen, (((1,), (1,)), ((), ())), preferred_element_type=jnp.float32)
        return raw / float(R)
    influence = lax.map(score_shard, shards).reshape(QUERIES, TRAIN)
    train_totals = lax.optimization_barrier(jnp.sum(influence, axis=0)) / math.sqrt(QUERIES)
    return (influence, train_totals)
```

```python
import functools
import math

import jax
import jax.numpy as jnp
from jax import lax
from jax.experimental import pallas as pl
from jax.experimental.pallas import tpu as pltpu
from jax.sharding import PartitionSpec as P

damping = 0.1
F32, BF16 = jnp.float32, jnp.bfloat16
CORES = 2
LANES = 128
HALF_CHUNKS = 8
Y_FIRST = 1
NN = (((1,), (0,)), ((), ()))
NT = (((1,), (1,)), ((), ()))


def dot(a, b, dims=NN, precision=None):
    return lax.dot_general(a, b, dims, precision=precision, preferred_element_type=F32)


def split(x):
    high = x.astype(BF16)
    return high, (x - high.astype(F32)).astype(BF16)


def kernel(Z, Y, train_ref, bo_ref, bi_ref, eo_ref, ei_ref, q_ref, infl_ref, tot_ref,
           buf, flat, queries, sums, q_sem, first_send, first_recv, got, shared,
           up_send, down_send, y_send, core_send, sum_send, sum_recv):
    n = Z * Y * CORES
    NC = HALF_CHUNKS
    nyf = Y_FIRST if Y > 1 else 0
    trains, side = train_ref.shape[0], train_ref.shape[1]
    rows = q_ref.shape[0]
    tiles = buf.shape[0]
    pack = side // tiles
    per_half = tiles // 2
    per = per_half // NC

    me = lax.axis_index("blk")
    core = lax.rem(me, CORES)
    chip = lax.div(me, CORES)
    y = lax.rem(chip, Y)
    z = lax.div(chip, Y)
    mine, other = core, 1 - core
    partner = chip * CORES + (1 - core)
    y_chip = z * Y + (1 - y)

    q_copy = pltpu.make_async_copy(q_ref, queries, q_sem)
    q_copy.start()

    barrier = pltpu.get_barrier_semaphore()

    def greet(step, carry):
        pl.semaphore_signal(barrier, inc=1, device_id={"blk": lax.rem(me + step, n)},
                            device_id_type=pl.DeviceIdType.MESH)
        return carry
    lax.fori_loop(1, n, greet, 0)

    bo, bi = bo_ref[...], bi_ref[...]
    bot = bo.astype(F32).T.astype(BF16)
    bit = bi.astype(F32).T.astype(BF16)
    weights = 1.0 / (jnp.broadcast_to(eo_ref[...], (side, side)).T * ei_ref[...] + damping)
    for t in range(trains):
        hi, lo = split(dot(train_ref[t], bi))
        turned = dot(bot, hi) + dot(bot, lo)
        hi, lo = split(turned * weights)
        back = dot(hi, bit) + dot(lo, bit)
        hi, lo = split(back)
        vector = dot(bo, hi) + dot(bo, lo)
        for c in range(side // LANES):
            flat[c, pl.ds(t, side, stride=trains), :] = vector[:, c * LANES:(c + 1) * LANES]
    for c in range(side // LANES):
        buf[:, me, :, c * LANES:(c + 1) * LANES] = (
            flat[c].astype(BF16).reshape(tiles, pack * trains, LANES))

    pl.semaphore_wait(barrier, n - 1)

    def remote(src, send, recv, device):
        return pltpu.make_async_remote_copy(
            src_ref=src, dst_ref=src, send_sem=send, recv_sem=recv,
            device_id={"blk": device}, device_id_type=pl.DeviceIdType.MESH)

    def span(half, k):
        return pl.ds(half * per_half + k * per, per)

    def first(half, k):
        i = half * NC + k
        return remote(buf.at[span(half, k), me], first_send.at[i], first_recv.at[i], partner)

    def first_wait(half, k):
        i = half * NC + k
        remote(buf.at[span(half, k), partner], first_send.at[i], first_recv.at[i], partner).wait_recv()

    def piece(half, o, k):
        return buf.at[span(half, k), pl.ds(o * CORES, CORES)]

    def to_chip(o, k, sems, target):
        i = o * NC + k
        return remote(piece(mine, o, k), sems.at[i], got.at[i], target * CORES + core)

    def up(o, k):
        return to_chip(o, k, up_send, chip + Y)

    def down(o, k):
        return to_chip(o, k, down_send, chip - Y)

    def across(o, k):
        return to_chip(o, k, y_send, y_chip)

    def core_copy(o, k):
        i = o * NC + k
        return remote(piece(mine, o, k), core_send.at[i], shared.at[i], partner)

    def arrived(o, k):
        i = o * NC + k
        remote(piece(mine, o, k), up_send.at[i], got.at[i], partner).wait_recv()

    def core_arrived(o, k):
        i = o * NC + k
        remote(piece(other, o, k), core_send.at[i], shared.at[i], partner).wait_recv()

    def chunks(low, high, body):
        def step(k, carry):
            body(k)
            return carry
        if high > low:
            lax.fori_loop(low, high, step, 0)

    has_up, has_down = z + 1 < Z, z > 0

    def start_z(o, k):
        pl.when(has_up)(lambda: up(o, k).start())
        pl.when(has_down)(lambda: down(o, k).start())

    chunks(0, NC, lambda k: first(other, k).start())
    chunks(0, NC, lambda k: first(mine, k).start())

    def begin(k):
        first_wait(mine, k)
        start_z(chip, k)
        if Y > 1:
            across(chip, k).start()
    chunks(0, NC, begin)

    if Y > 1:
        def cross(k):
            arrived(y_chip, k)
            start_z(y_chip, k)
            core_copy(y_chip, k).start()
        chunks(0, nyf, cross)

    def from_y(o, k):
        arrived(o, k)
        core_copy(o, k).start()

    def side_step(d, sign, k):
        oz = z + sign * d
        inside = oz >= 0 if sign < 0 else oz < Z
        more = has_up if sign < 0 else has_down

        @pl.when(inside)
        def _():
            def forward(o):
                arrived(o, k)

                @pl.when(more)
                def _():
                    (up if sign < 0 else down)(o, k).start()
            o = oz * Y + y
            forward(o)
            if Y > 1:
                pl.when(k >= nyf)(lambda: across(o, k).start())
            core_copy(o, k).start()
            if nyf:
                @pl.when(k < nyf)
                def _():
                    far = oz * Y + (1 - y)
                    forward(far)
                    core_copy(far, k).start()

    def y_side(d, sign, k):
        oz = z + sign * d
        inside = oz >= 0 if sign < 0 else oz < Z
        pl.when(inside)(lambda: from_y(oz * Y + (1 - y), k))

    def plane(d, carry):
        def one(k):
            side_step(d, -1, k)
            side_step(d, 1, k)
            if Y > 1:
                @pl.when(k >= nyf)
                def _():
                    @pl.when(d == 1)
                    def _():
                        from_y(y_chip, k)

                    @pl.when(d > 1)
                    def _():
                        y_side(d - 1, -1, k)
                        y_side(d - 1, 1, k)
        chunks(0, NC, one)
        return carry
    lax.fori_loop(1, Z, plane, 0)

    width = n * pack * trains

    def score(half, k, acc):
        accs = list(acc)
        for i in range(per):
            tile = half * per_half + k * per + i
            block = buf[tile].reshape(width, side)
            for a in range(pack):
                col = pl.multiple_of((tile * pack + a) * side, side)
                accs[a] = accs[a] + dot(queries[:, pl.ds(col, side)], block, NT)
        return tuple(accs)

    def others_arrived(k):
        first_wait(other, k)

        def one(s, carry):
            core_arrived(lax.rem(chip + s, Z * Y), k)
            return carry
        lax.fori_loop(1, Z * Y, one, 0)

    q_copy.wait()

    def last(k, acc):
        if Y > 1:
            @pl.when(k >= nyf)
            def _():
                if Z == 1:
                    from_y(y_chip, k)
                else:
                    y_side(Z - 1, -1, k)
                    y_side(Z - 1, 1, k)
        return score(mine, k, acc)

    def rest(k, acc):
        others_arrived(k)
        return score(other, k, acc)

    acc = tuple(jnp.zeros((rows, width), F32) for _ in range(pack))
    acc = last(0, acc)

    def both(k, acc):
        return rest(k - 1, last(k, acc))
    acc = lax.fori_loop(1, NC, both, acc)
    acc = rest(NC - 1, acc)

    column = lax.broadcasted_iota(jnp.int32, (1, width), 1)
    which = lax.rem(lax.div(column, trains), pack)
    merged = acc[0]
    for a in range(1, pack):
        merged = jnp.where(which == a, acc[a], merged)
    source = lax.broadcasted_iota(jnp.int32, (width, n * trains), 0)
    place = lax.div(source, pack * trains) * trains + lax.rem(source, trains)
    target = lax.broadcasted_iota(jnp.int32, (width, n * trains), 1)
    pick = jnp.where(place == target, 1.0, 0.0).astype(F32)
    influence = dot(merged, pick, precision=lax.Precision.HIGHEST) / float(side)
    infl_ref[...] = influence

    sums[me] = jnp.broadcast_to(jnp.sum(influence, axis=0, keepdims=True), sums.shape[1:])

    def sum_copy(step):
        to = lax.rem(me + step, n)
        return remote(sums.at[me], sum_send.at[step], sum_recv.at[me], to)

    def sum_wait(step):
        src = lax.rem(me + step, n)
        remote(sums.at[src], sum_send.at[step], sum_recv.at[src], src).wait_recv()

    chunks(1, n, lambda s: sum_copy(s).start())

    chunks(0, NC, lambda k: first(other, k).wait_send())
    chunks(0, NC, lambda k: first(mine, k).wait_send())

    def own_left(o, k):
        pl.when(has_up)(lambda: up(o, k).wait_send())
        pl.when(has_down)(lambda: down(o, k).wait_send())

    def left(k):
        own_left(chip, k)
        if Y > 1:
            across(chip, k).wait_send()
            pl.when(k < nyf)(lambda: own_left(y_chip, k))
            core_copy(y_chip, k).wait_send()

        def one(oz, carry):
            near, far = oz * Y + y, oz * Y + (1 - y)

            @pl.when(oz != z)
            def _():
                core_copy(near, k).wait_send()
                pl.when((oz < z) & has_up)(lambda: up(near, k).wait_send())
                pl.when((oz > z) & has_down)(lambda: down(near, k).wait_send())
                if Y > 1:
                    core_copy(far, k).wait_send()
                    pl.when(k >= nyf)(lambda: across(near, k).wait_send())
                    pl.when((k < nyf) & (oz < z) & has_up)(lambda: up(far, k).wait_send())
                    pl.when((k < nyf) & (oz > z) & has_down)(lambda: down(far, k).wait_send())
            return carry
        lax.fori_loop(0, Z, one, 0)
    chunks(0, NC, left)

    chunks(1, n, sum_wait)
    total = jnp.sum(sums[...], axis=0)
    tot_ref[...] = total * (1.0 / math.sqrt(rows * n))
    chunks(1, n, lambda s: sum_copy(s).wait_send())


def grid_of(mesh):
    n = mesh.shape["blk"]
    chips = n // CORES
    try:
        group = mesh.devices.reshape(-1, n)[0]
        Y = len({tuple(d.coords[:2]) for d in group})
    except AttributeError:
        Y = 2 if chips % 2 == 0 else 1
    return chips // Y, Y


def local(Z, Y, query_grads, train_grads, basis_out, basis_in, eigen_out, eigen_in):
    side = basis_in.shape[0]
    trains = train_grads.shape[0]
    rows = query_grads.shape[0]
    n = Z * Y * CORES
    pack = 16 // trains
    tiles = side // pack
    pieces = Z * Y * HALF_CHUNKS
    dma = pltpu.SemaphoreType.DMA
    vmem = pl.BlockSpec(memory_space=pltpu.VMEM)
    influence, totals = pl.pallas_call(
        functools.partial(kernel, Z, Y),
        out_shape=(jax.ShapeDtypeStruct((rows, n * trains), F32),
                   jax.ShapeDtypeStruct((8, n * trains), F32)),
        in_specs=[vmem] * 5 + [pl.BlockSpec(memory_space=pl.ANY)],
        out_specs=(vmem, vmem),
        scratch_shapes=[
            pltpu.VMEM((tiles, n, pack * trains, side), BF16),
            pltpu.VMEM((side // LANES, side * trains, LANES), F32),
            pltpu.VMEM(query_grads.shape, BF16),
            pltpu.VMEM((n, 8, n * trains), F32),
            dma(()),
            dma((2 * HALF_CHUNKS,)), dma((2 * HALF_CHUNKS,)),
            dma((pieces,)), dma((pieces,)),
            dma((pieces,)), dma((pieces,)), dma((pieces,)), dma((pieces,)),
            dma((n,)), dma((n,)),
        ],
        compiler_params=pltpu.CompilerParams(
            collective_id=0, has_side_effects=True, vmem_limit_bytes=60 * 2**20),
        cost_estimate=pl.CostEstimate(
            flops=4 * rows * side * side * n * trains,
            bytes_accessed=2 * rows * side * side, transcendentals=0),
    )(train_grads.reshape(trains, side, side), basis_out, basis_in,
      eigen_out.reshape(1, side), eigen_in.reshape(1, side), query_grads)
    own = lax.dynamic_slice_in_dim(totals[0], lax.axis_index("blk") * trains, trains)
    return influence, own


def solution(mesh):
    Z, Y = grid_of(mesh)
    return jax.shard_map(
        functools.partial(local, Z, Y),
        mesh=mesh,
        in_specs=(P(("groups", "blk"), None), P(("groups", "blk"), None), P(), P(), P(), P()),
        out_specs=(P(("groups", "blk"), None), P(("groups", "blk"))),
        check_vma=False,
    )
```

```python
import functools
import math

import jax
import jax.numpy as jnp
from jax import lax
from jax.experimental import pallas as pl
from jax.experimental.pallas import tpu as pltpu
from jax.sharding import PartitionSpec as P

damping = 0.1
F32, BF16 = jnp.float32, jnp.bfloat16
CORES = 2
LANES = 128
HALF_CHUNKS = 8
Y_FIRST = 1
NN = (((1,), (0,)), ((), ()))
NT = (((1,), (1,)), ((), ()))


def dot(a, b, dims=NN, precision=None):
    return lax.dot_general(a, b, dims, precision=precision, preferred_element_type=F32)


def split(x):
    high = x.astype(BF16)
    return high, (x - high.astype(F32)).astype(BF16)


def kernel(Z, Y, train_ref, bo_ref, bi_ref, eo_ref, ei_ref, q_ref, infl_ref, tot_ref,
           buf, flat, queries, sums, q_sem, first_send, first_recv, got, shared,
           up_send, down_send, y_send, core_send, sum_send, sum_recv):
    n = Z * Y * CORES
    NC = HALF_CHUNKS
    nyf = Y_FIRST if Y > 1 else 0
    trains, side = train_ref.shape[0], bo_ref.shape[0]
    rows = q_ref.shape[0]
    tiles = buf.shape[0]
    pack = side // tiles
    per_half = tiles // 2
    per = per_half // NC

    me = lax.axis_index("blk")
    core = lax.rem(me, CORES)
    chip = lax.div(me, CORES)
    y = lax.rem(chip, Y)
    z = lax.div(chip, Y)
    mine, other = core, 1 - core
    partner = chip * CORES + (1 - core)
    y_chip = z * Y + (1 - y)

    q_copy = pltpu.make_async_copy(q_ref, queries, q_sem)
    q_copy.start()

    barrier = pltpu.get_barrier_semaphore()

    def greet(step, carry):
        pl.semaphore_signal(barrier, inc=1, device_id={"blk": lax.rem(me + step, n)},
                            device_id_type=pl.DeviceIdType.MESH)
        return carry
    lax.fori_loop(1, n, greet, 0)

    bo, bi = bo_ref[...], bi_ref[...]
    bot = bo.astype(F32).T.astype(BF16)
    bit = bi.astype(F32).T.astype(BF16)
    weights = 1.0 / (jnp.broadcast_to(eo_ref[...], (side, side)).T * ei_ref[...] + damping)
    halves = range(side // LANES)
    for a in range(side):
        for c in halves:
            flat[c, a * trains:(a + 1) * trains, :] = (
                train_ref[:, a * side + c * LANES:a * side + (c + 1) * LANES].astype(F32))
    for t in range(trains):
        matrix = jnp.concatenate([flat[c, pl.ds(t, side, stride=trains), :] for c in halves], axis=1)
        hi, lo = split(dot(matrix.astype(BF16), bi))
        turned = dot(bot, hi) + dot(bot, lo)
        hi, lo = split(turned * weights)
        back = dot(hi, bit) + dot(lo, bit)
        hi, lo = split(back)
        vector = dot(bo, hi) + dot(bo, lo)
        for c in range(side // LANES):
            flat[c, pl.ds(t, side, stride=trains), :] = vector[:, c * LANES:(c + 1) * LANES]
    for c in range(side // LANES):
        buf[:, me, :, c * LANES:(c + 1) * LANES] = (
            flat[c].astype(BF16).reshape(tiles, pack * trains, LANES))

    pl.semaphore_wait(barrier, n - 1)

    def remote(src, send, recv, device):
        return pltpu.make_async_remote_copy(
            src_ref=src, dst_ref=src, send_sem=send, recv_sem=recv,
            device_id={"blk": device}, device_id_type=pl.DeviceIdType.MESH)

    def span(half, k):
        return pl.ds(half * per_half + k * per, per)

    def first(half, k):
        i = half * NC + k
        return remote(buf.at[span(half, k), me], first_send.at[i], first_recv.at[i], partner)

    def first_wait(half, k):
        i = half * NC + k
        remote(buf.at[span(half, k), partner], first_send.at[i], first_recv.at[i], partner).wait_recv()

    def piece(half, o, k):
        return buf.at[span(half, k), pl.ds(o * CORES, CORES)]

    def to_chip(o, k, sems, target):
        i = o * NC + k
        return remote(piece(mine, o, k), sems.at[i], got.at[i], target * CORES + core)

    def up(o, k):
        return to_chip(o, k, up_send, chip + Y)

    def down(o, k):
        return to_chip(o, k, down_send, chip - Y)

    def across(o, k):
        return to_chip(o, k, y_send, y_chip)

    def core_copy(o, k):
        i = o * NC + k
        return remote(piece(mine, o, k), core_send.at[i], shared.at[i], partner)

    def arrived(o, k):
        i = o * NC + k
        remote(piece(mine, o, k), up_send.at[i], got.at[i], partner).wait_recv()

    def core_arrived(o, k):
        i = o * NC + k
        remote(piece(other, o, k), core_send.at[i], shared.at[i], partner).wait_recv()

    def chunks(low, high, body):
        def step(k, carry):
            body(k)
            return carry
        if high > low:
            lax.fori_loop(low, high, step, 0)

    has_up, has_down = z + 1 < Z, z > 0

    def start_z(o, k):
        pl.when(has_up)(lambda: up(o, k).start())
        pl.when(has_down)(lambda: down(o, k).start())

    chunks(0, NC, lambda k: first(other, k).start())
    chunks(0, NC, lambda k: first(mine, k).start())

    near = NC - nyf

    def cross_first(k):
        first_wait(mine, k)
        across(chip, k).start()
    chunks(near, NC, cross_first)

    def begin(k):
        first_wait(mine, k)
        start_z(chip, k)
        if Y > 1:
            across(chip, k).start()
    chunks(0, near, begin)
    chunks(near, NC, lambda k: start_z(chip, k))

    def cross(k):
        arrived(y_chip, k)
        start_z(y_chip, k)
        core_copy(y_chip, k).start()
    chunks(near, NC, cross)

    def from_y(o, k):
        arrived(o, k)
        core_copy(o, k).start()

    def pass_on(d, k, column, to_y):
        def one(oz, inside, more, onward):
            @pl.when(inside)
            def _():
                o = oz * Y + column
                arrived(o, k)
                pl.when(more)(lambda: onward(o, k).start())
                if to_y:
                    across(o, k).start()
                core_copy(o, k).start()
        one(z - d, z - d >= 0, has_up, up)
        one(z + d, z + d < Z, has_down, down)

    def y_pieces(d, k):
        @pl.when(d == 0)
        def _():
            from_y(y_chip, k)

        @pl.when(d > 0)
        def _():
            pl.when(z - d >= 0)(lambda: from_y((z - d) * Y + (1 - y), k))
            pl.when(z + d < Z)(lambda: from_y((z + d) * Y + (1 - y), k))

    def plane(d, carry):
        chunks(0, near, lambda k: pass_on(d, k, y, Y > 1))
        chunks(near, NC, lambda k: pass_on(d, k, y, False))
        chunks(near, NC, lambda k: pass_on(d, k, 1 - y, False))
        if Y > 1:
            chunks(0, near, lambda k: y_pieces(d - 1, k))
        return carry
    lax.fori_loop(1, Z, plane, 0)

    width = n * pack * trains

    def score(half, k, acc):
        accs = list(acc)
        for i in range(per):
            tile = half * per_half + k * per + i
            block = buf[tile].reshape(width, side)
            for a in range(pack):
                col = pl.multiple_of((tile * pack + a) * side, side)
                accs[a] = accs[a] + dot(queries[:, pl.ds(col, side)], block, NT)
        return tuple(accs)

    def others_arrived(k):
        first_wait(other, k)

        def one(s, carry):
            core_arrived(lax.rem(chip + s, Z * Y), k)
            return carry
        lax.fori_loop(1, Z * Y, one, 0)

    q_copy.wait()

    def last(k, acc):
        if Y > 1:
            pl.when(k < near)(lambda: y_pieces(Z - 1, k))
        return score(mine, k, acc)

    def rest(k, acc):
        others_arrived(k)
        return score(other, k, acc)

    acc = tuple(jnp.zeros((rows, width), F32) for _ in range(pack))
    acc = last(0, acc)

    def both(k, acc):
        return rest(k - 1, last(k, acc))
    acc = lax.fori_loop(1, NC, both, acc)
    acc = rest(NC - 1, acc)

    column = lax.broadcasted_iota(jnp.int32, (1, width), 1)
    which = lax.rem(lax.div(column, trains), pack)
    merged = acc[0]
    for a in range(1, pack):
        merged = jnp.where(which == a, acc[a], merged)
    source = lax.broadcasted_iota(jnp.int32, (width, n * trains), 0)
    place = lax.div(source, pack * trains) * trains + lax.rem(source, trains)
    target = lax.broadcasted_iota(jnp.int32, (width, n * trains), 1)
    pick = jnp.where(place == target, 1.0, 0.0).astype(F32)
    influence = dot(merged, pick, precision=lax.Precision.HIGHEST) / float(side)
    infl_ref[...] = influence

    sums[me] = jnp.broadcast_to(jnp.sum(influence, axis=0, keepdims=True), sums.shape[1:])

    def sum_copy(step):
        to = lax.rem(me + step, n)
        return remote(sums.at[me], sum_send.at[step], sum_recv.at[me], to)

    def sum_wait(step):
        src = lax.rem(me + step, n)
        remote(sums.at[src], sum_send.at[step], sum_recv.at[src], src).wait_recv()

    chunks(1, n, lambda s: sum_copy(s).start())

    chunks(0, NC, lambda k: first(other, k).wait_send())
    chunks(0, NC, lambda k: first(mine, k).wait_send())

    def own_left(o, k):
        pl.when(has_up)(lambda: up(o, k).wait_send())
        pl.when(has_down)(lambda: down(o, k).wait_send())

    def left(k):
        own_left(chip, k)
        if Y > 1:
            across(chip, k).wait_send()
            pl.when(k >= near)(lambda: own_left(y_chip, k))
            core_copy(y_chip, k).wait_send()

        def one(oz, carry):
            same, far = oz * Y + y, oz * Y + (1 - y)

            @pl.when(oz != z)
            def _():
                core_copy(same, k).wait_send()
                pl.when((oz < z) & has_up)(lambda: up(same, k).wait_send())
                pl.when((oz > z) & has_down)(lambda: down(same, k).wait_send())
                if Y > 1:
                    core_copy(far, k).wait_send()
                    pl.when(k < near)(lambda: across(same, k).wait_send())
                    pl.when((k >= near) & (oz < z) & has_up)(lambda: up(far, k).wait_send())
                    pl.when((k >= near) & (oz > z) & has_down)(lambda: down(far, k).wait_send())
            return carry
        lax.fori_loop(0, Z, one, 0)
    chunks(0, NC, left)

    chunks(1, n, sum_wait)
    total = jnp.sum(sums[...], axis=0)
    tot_ref[...] = total * (1.0 / math.sqrt(rows * n))
    chunks(1, n, lambda s: sum_copy(s).wait_send())


def grid_of(mesh):
    n = mesh.shape["blk"]
    chips = n // CORES
    try:
        group = mesh.devices.reshape(-1, n)[0]
        Y = len({tuple(d.coords[:2]) for d in group})
    except AttributeError:
        Y = 2 if chips % 2 == 0 else 1
    return chips // Y, Y


def local(Z, Y, query_grads, train_grads, basis_out, basis_in, eigen_out, eigen_in):
    side = basis_in.shape[0]
    trains = train_grads.shape[0]
    rows = query_grads.shape[0]
    n = Z * Y * CORES
    pack = 16 // trains
    tiles = side // pack
    pieces = Z * Y * HALF_CHUNKS
    dma = pltpu.SemaphoreType.DMA
    vmem = pl.BlockSpec(memory_space=pltpu.VMEM)
    influence, totals = pl.pallas_call(
        functools.partial(kernel, Z, Y),
        out_shape=(jax.ShapeDtypeStruct((rows, n * trains), F32),
                   jax.ShapeDtypeStruct((8, n * trains), F32)),
        in_specs=[vmem] * 5 + [pl.BlockSpec(memory_space=pl.ANY)],
        out_specs=(vmem, vmem),
        scratch_shapes=[
            pltpu.VMEM((tiles, n, pack * trains, side), BF16),
            pltpu.VMEM((side // LANES, side * trains, LANES), F32),
            pltpu.VMEM(query_grads.shape, BF16),
            pltpu.VMEM((n, 8, n * trains), F32),
            dma(()),
            dma((2 * HALF_CHUNKS,)), dma((2 * HALF_CHUNKS,)),
            dma((pieces,)), dma((pieces,)),
            dma((pieces,)), dma((pieces,)), dma((pieces,)), dma((pieces,)),
            dma((n,)), dma((n,)),
        ],
        compiler_params=pltpu.CompilerParams(
            collective_id=0, has_side_effects=True, vmem_limit_bytes=60 * 2**20),
        cost_estimate=pl.CostEstimate(
            flops=4 * rows * side * side * n * trains,
            bytes_accessed=2 * rows * side * side, transcendentals=0),
    )(train_grads, basis_out, basis_in,
      eigen_out.reshape(1, side), eigen_in.reshape(1, side), query_grads)
    own = lax.dynamic_slice_in_dim(totals[0], lax.axis_index("blk") * trains, trains)
    return influence, own


def solution(mesh):
    Z, Y = grid_of(mesh)
    return jax.shard_map(
        functools.partial(local, Z, Y),
        mesh=mesh,
        in_specs=(P(("groups", "blk"), None), P(("groups", "blk"), None), P(), P(), P(), P()),
        out_specs=(P(("groups", "blk"), None), P(("groups", "blk"))),
        check_vma=False,
    )
```
